32 devices in a mesh: groups: 2 (over x), ep: 16 (over z, y, core).
Axes of the slice: x: 2, y: 2, z: 4, core: 2. Of those that a mesh axis runs over, the one named last changes fastest.
Arguments:
- resid: bfloat16 [4096, 2048], P(('groups', 'ep')), parts along dimension 0, may hold values from -12 to 12
- norm_gain: float32 [2048], replicated, may hold values from 0.1 to 1.9
- expert_ids: int32 [4096, 8], P(('groups', 'ep')), parts along dimension 0, may hold values from 0 to 15, as said below
- route_weights: float32 [4096, 8], P(('groups', 'ep')), parts along dimension 0, may hold values from 0.05 to 1
- w_in: bfloat16 [16, 2048, 1536], P('ep'), may hold values from -0.125 to 0.125
- w_out: bfloat16 [16, 768, 2048], P('ep'), may hold values from -0.21875 to 0.21875
Outputs:
- layer_out: bfloat16 [4096, 2048], P(('groups', 'ep')), parts along dimension 0
The draws below stay inside these ranges and needn't reach their ends.
There are 2 independent parts, one for each index of `groups`. The reference program is written for one: setup_inputs(seed, part) draws one part's arguments, and reference() takes and returns one part's arrays. A program takes and returns all parts, laid end to end along the dimension named above; an argument that names none is the same for every part. Nothing has to cross between parts.
Inputs may be any that keep to these rules, and one draw needn't show every extreme that they name: `expert_ids`: each row names 8 different experts. Among the rows of one device no expert is named by more than 96 rows, and in every draw one expert is named by exactly 96 rows of every device.
All inputs are finite; a program needn't handle non-finite values.
Results may differ from the reference program's by a relative error of at most 0.0053.
Values may be sent and summed in bfloat16 or wider, within the bound.
No kernel may reach another device: no remote copies, remote signals or barrier semaphores. Data moves between devices by JAX's collectives and lax.ppermute only.
A program may use at most 128 MiB of HBM per device.

```python
import math
import jax
import jax.numpy as jnp
from jax import lax

D = 2048
TOPK = 8
FF = 768
TOK_DEV = 128
EXPERTS = 16
TOKENS = 2048
CAP = 96


def draw_resid(key, part):
    first_key, second_key, third_key = jax.random.split(key, 3)
    base = jnp.clip(jax.random.normal(first_key, (TOKENS, D), jnp.float32), -4.0, 4.0)
    row_scale = jnp.exp(jax.random.uniform(second_key, (TOKENS, 1), jnp.float32, jnp.log(0.1), jnp.log(1.0)))
    column_scale = jnp.exp(jax.random.uniform(third_key, (1, D), jnp.float32, jnp.log(0.3), jnp.log(3.0)))
    return (base * row_scale * column_scale).astype(jnp.bfloat16)


def draw_expert_ids(key, part):
    blocks = TOKENS // TOK_DEV
    slot_total = EXPERTS * CAP
    chosen_count = TOK_DEV * TOPK
    favour = jax.random.randint(jax.random.fold_in(key, 11), (EXPERTS,), 0, slot_total)
    hot_expert = jax.random.randint(jax.random.fold_in(key, 12), (), 0, EXPERTS)
    expert_of = jnp.arange(slot_total, dtype=jnp.int32) // CAP
    order_key = slot_total - 1 - jnp.arange(slot_total, dtype=jnp.int32)

    def one_block(block):
        block_key = jax.random.fold_in(key, block + 100)
        noise = jax.random.randint(jax.random.fold_in(block_key, 1), (slot_total,), 0, slot_total)
        score = noise + favour[expert_of] + jnp.where(expert_of == hot_expert, 2 * slot_total, 0)
        unused, picked = lax.top_k(score * slot_total + order_key, chosen_count)
        marked = jnp.zeros((slot_total,), jnp.int32).at[picked].set(1)
        unused_too, ordered = lax.top_k(marked * slot_total + order_key, chosen_count)
        listed = (ordered // CAP).reshape(TOPK, TOK_DEV).T
        shuffle = jax.random.permutation(jax.random.fold_in(block_key, 2), TOK_DEV)
        return listed[shuffle]
    drawn = jax.vmap(one_block)(jnp.arange(blocks, dtype=jnp.int32))
    return drawn.reshape(TOKENS, TOPK).astype(jnp.int32)


def levels(stream_key, shape, cuts, smallest, top_value):
    loudness, own = 1.0, jax.random.fold_in(stream_key, 6)
    for dim, parts in cuts:
        heights = jnp.exp(jax.random.uniform(jax.random.fold_in(own, dim), (parts,), jnp.float32, smallest / len(cuts), top_value / len(cuts)))
        loudness = loudness * jnp.repeat(heights, shape[dim] // parts).reshape([-1 if axis == dim else 1 for axis in range(len(shape))])
    return loudness


def scatter_about(own_key, shape, width, limit, cuts=(), held_as=jnp.bfloat16):
    level = levels(own_key, shape, cuts, -0.22, 0.18) if cuts else 1.0
    values = jax.random.normal(own_key, shape, jnp.float32) * width * level
    return jnp.minimum(jnp.maximum(values, -limit), limit).astype(held_as)


def setup_inputs(seed: int = 0, part: int = 0) -> dict:
    key_list = jax.random.split(jax.random.key(seed), 7)
    part_keys = jax.random.split(jax.random.fold_in(key_list[6], part), 7)
    return {
        "resid": draw_resid(jax.random.fold_in(jax.random.fold_in(key_list[6], part), 71), part),
        "norm_gain": jnp.clip(1.0 + 0.18 * jax.random.normal(key_list[1], (D,), jnp.float32), 0.1, 1.9),
        "expert_ids": draw_expert_ids(jax.random.fold_in(jax.random.fold_in(key_list[6], part), 71), part),
        "route_weights": jnp.clip(jnp.exp(math.log(1.0) - 2.9957323 * jax.random.uniform(part_keys[3], (TOKENS, TOPK), jnp.float32) ** levels(part_keys[3], (TOKENS, TOPK), ((0, 16),), -0.2, 0.2)), 0.05, 1.0),
        "w_in": scatter_about(key_list[4], (EXPERTS, D, 2 * FF), D ** -0.5, 0.125, ((0, 16),)),
        "w_out": scatter_about(key_list[5], (EXPERTS, FF, D), FF ** -0.5, 0.21875, ((0, 16),)),
    }


def apply_expert(block_rows, weight_in, weight_out):
    projected = jnp.dot(block_rows, weight_in, preferred_element_type=jnp.float32)
    gate_part = projected[:, :FF]
    up_part = projected[:, FF:]
    activated = (jax.nn.silu(gate_part) * up_part).astype(jnp.bfloat16)
    return jnp.dot(activated, weight_out, preferred_element_type=jnp.float32).astype(jnp.bfloat16)

def reference(resid, norm_gain, expert_ids, route_weights, w_in, w_out):
    token_count, model_width = resid.shape
    blocks = token_count // TOK_DEV
    resid_wide = resid.astype(jnp.float32)
    scale = lax.rsqrt(lax.optimization_barrier(jnp.mean(resid_wide * resid_wide, axis=-1, keepdims=True)) + 1e-06)
    normed = (resid_wide * scale * norm_gain).astype(jnp.bfloat16)
    mix_weights = route_weights / lax.optimization_barrier(jnp.sum(route_weights, axis=-1, keepdims=True))
    flat_ids = expert_ids.reshape(blocks, TOK_DEV * TOPK).astype(jnp.int32)
    onehot = (flat_ids[:, :, None] == jnp.arange(EXPERTS, dtype=jnp.int32)[None, None, :]).astype(jnp.int32)
    position = lax.optimization_barrier(jnp.sum((jnp.cumsum(onehot, axis=1) - onehot) * onehot, axis=-1)).astype(jnp.int32)
    column = (jnp.arange(blocks, dtype=jnp.int32)[:, None] * CAP + position).astype(jnp.int32)
    token_of = jnp.repeat(jnp.arange(token_count, dtype=jnp.int32), TOPK).reshape(blocks, TOK_DEV * TOPK)
    table = jnp.zeros((EXPERTS, blocks * CAP), jnp.int32).at[flat_ids, column].set(token_of)
    weight_table = jnp.zeros((EXPERTS, blocks * CAP), jnp.float32).at[flat_ids, column].set(mix_weights.reshape(blocks, TOK_DEV * TOPK))

    def one_expert(total, inputs):
        weight_in, weight_out, token_rows, row_weights = inputs
        outputs = apply_expert(normed[token_rows], weight_in, weight_out)
        total = total.at[token_rows].add(row_weights[:, None] * outputs.astype(jnp.float32))
        return (total, None)
    total, _ = lax.scan(one_expert, jnp.zeros((token_count, model_width), jnp.float32), (w_in, w_out, table, weight_table))
    return (resid_wide + total).astype(jnp.bfloat16)
```

```python
import functools

import jax
import jax.numpy as jnp
from jax import lax
from jax.experimental import pallas as pl
from jax.experimental.pallas import tpu as pltpu
from jax.sharding import PartitionSpec as P

LANES = 128
CORES = 2


def ring_of(chips):
    order = list(range(0, chips, 2)) + list(range(1, chips, 2))[::-1]
    right, left, swap = [], [], []
    for place, chip in enumerate(order):
        after = order[(place + 1) % chips]
        for core in range(CORES):
            right.append((chip * CORES + core, after * CORES + core))
            left.append((after * CORES + core, chip * CORES + core))
            swap.append((chip * CORES + core, chip * CORES + 1 - core))
    return right, left, swap


def pack_kernel(experts, resid_ref, gain_ref, ids_ref, route_ref, out_ref):
    rows, width = resid_ref.shape
    lanes = out_ref.shape[1] - width
    wide = resid_ref[...].astype(jnp.float32)
    scale = lax.rsqrt(jnp.mean(wide * wide, axis=-1, keepdims=True) + 1e-06)
    out_ref[:, :width] = (wide * scale * gain_ref[...]).astype(jnp.bfloat16)
    route = route_ref[...]
    mix = route / jnp.sum(route, axis=-1, keepdims=True)
    ids = ids_ref[...]
    lane = lax.broadcasted_iota(jnp.int32, (rows, lanes), 1)
    expert = jnp.where(lane < experts, lane, lane - experts)
    table = jnp.zeros((rows, lanes), jnp.float32)
    for k in range(ids.shape[1]):
        table += jnp.where(ids[:, k : k + 1] == expert, mix[:, k : k + 1], 0.0)
    high = table.astype(jnp.bfloat16)
    low = (table - high.astype(jnp.float32)).astype(jnp.bfloat16)
    out_ref[:, width:] = jnp.where(lane < experts, high.astype(jnp.float32), low.astype(jnp.float32)).astype(
        jnp.bfloat16
    )


def pack(resid, norm_gain, expert_ids, route_weights, experts):
    rows, width = resid.shape
    lanes = -(-2 * experts // LANES) * LANES
    return pl.pallas_call(
        functools.partial(pack_kernel, experts),
        out_shape=jax.ShapeDtypeStruct((rows, width + lanes), jnp.bfloat16),
        compiler_params=pltpu.CompilerParams(vmem_limit_bytes=32 * 2**20),
        name="pack_rows",
    )(resid, norm_gain.reshape(1, width), expert_ids, route_weights)


def expert_kernel(count, experts, hidden_steps, *refs):
    own_ref = refs[0]
    blocks = refs[1 : 1 + count]
    gate_ref, up_ref, down_ref = refs[1 + count : 4 + count]
    outs = refs[4 + count : 6 + count]
    rows_ref, active_ref, weight_ref = refs[6 + count :]
    step = pl.program_id(0)
    total, width = rows_ref.shape
    half = total // 2
    tile = gate_ref.shape[1]

    @pl.when(step == 0)
    def _():
        start = 0
        for block in blocks:
            size = block.shape[0]
            rows_ref[start : start + size, :] = block[:, :width]
            table = block[:, width:].astype(jnp.float32)
            lane = lax.broadcasted_iota(jnp.int32, table.shape, 1)
            mine = (lane == own_ref[0]) | (lane == own_ref[0] + experts)
            weight = jnp.sum(jnp.where(mine, table, 0.0), axis=1, keepdims=True)
            weight_ref[start : start + size, :] = jnp.broadcast_to(weight, (size, LANES))
            start += size

    @pl.when(step < hidden_steps)
    def _():
        rows = rows_ref[...]
        gate = jnp.dot(rows, gate_ref[...], preferred_element_type=jnp.float32)
        up = jnp.dot(rows, up_ref[...], preferred_element_type=jnp.float32)
        value = (gate / (1.0 + jnp.exp(-gate)) * up).astype(jnp.bfloat16)
        for j in range(hidden_steps):

            @pl.when(step == j)
            def _():
                active_ref[:, j * tile : (j + 1) * tile] = value

    @pl.when(step >= hidden_steps)
    def _():
        produced = jnp.dot(active_ref[...], down_ref[...], preferred_element_type=jnp.float32)
        produced = produced.astype(jnp.bfloat16).astype(jnp.float32)
        weight = weight_ref[:, :1]
        mixed = jnp.where(weight == 0.0, 0.0, produced * weight).astype(jnp.bfloat16)
        outs[0][...] = mixed[:half]
        outs[1][...] = mixed[half:]


def apply_expert(own, blocks, w_in, w_out, experts):
    hidden, width = w_out.shape[1:]
    packed = blocks[0].shape[1]
    total = sum(block.shape[0] for block in blocks)
    tile = 256 if hidden % 256 == 0 else LANES
    hidden_steps = hidden // tile
    out_tile = 512 if width % 512 == 0 else LANES
    out_steps = width // out_tile
    late = lambda j: jnp.maximum(j - hidden_steps, 0)
    early = lambda j: jnp.minimum(j, hidden_steps - 1)
    return pl.pallas_call(
        functools.partial(expert_kernel, len(blocks), experts, hidden_steps),
        grid=(hidden_steps + out_steps,),
        in_specs=[pl.BlockSpec(memory_space=pltpu.SMEM)]
        + [pl.BlockSpec(block.shape, lambda j: (0, 0)) for block in blocks]
        + [
            pl.BlockSpec((None, width, tile), lambda j: (0, 0, early(j))),
            pl.BlockSpec((None, width, tile), lambda j: (0, 0, early(j) + hidden_steps)),
            pl.BlockSpec((None, hidden, out_tile), lambda j: (0, 0, late(j))),
        ],
        out_specs=[pl.BlockSpec((total // 2, out_tile), lambda j: (0, late(j)))] * 2,
        out_shape=[jax.ShapeDtypeStruct((total // 2, width), jnp.bfloat16)] * 2,
        scratch_shapes=[
            pltpu.VMEM((total, width), jnp.bfloat16),
            pltpu.VMEM((total, hidden), jnp.bfloat16),
            pltpu.VMEM((total, LANES), jnp.float32),
        ],
        compiler_params=pltpu.CompilerParams(
            dimension_semantics=("arbitrary",), vmem_limit_bytes=40 * 2**20
        ),
        cost_estimate=pl.CostEstimate(
            flops=6 * total * width * hidden,
            bytes_accessed=6 * width * hidden + 4 * total * (packed + width),
            transcendentals=total * hidden,
        ),
        name="expert_rows",
    )(own, *blocks, w_in, w_in, w_out)


def local(resid, norm_gain, expert_ids, route_weights, w_in, w_out):
    rows, width = resid.shape
    devices = lax.axis_size("ep")
    chips = devices // CORES
    right, left, swap = ring_of(chips)
    own = lax.axis_index("ep").reshape(1).astype(jnp.int32)
    half = rows // 2
    full_steps = (chips - 1) // 2
    opposite = chips % 2 == 0

    def move(array, perm):
        return lax.ppermute(array, "ep", perm)

    def expert(blocks):
        return apply_expert(own, blocks, w_in, w_out, devices)

    block = pack(resid, norm_gain, expert_ids, route_weights, devices)

    rightward, leftward = [block], [block]
    for _ in range(full_steps):
        rightward.append(move(rightward[-1], right))
        leftward.append(move(leftward[-1], left))
    if opposite:
        far_top = move(rightward[-1][:half], right)
        far_bottom = move(leftward[-1][half:], left)

    batches = [[block, move(block, swap)]]
    for k in range(1, full_steps + 1):
        mine = [rightward[k], leftward[k]]
        batches.append(mine + [move(part, swap) for part in mine])
    if opposite:
        mine = [far_top, far_bottom]
        batches.append(mine + [move(part, swap) for part in mine])

    sums = []
    for batch in batches:
        keep, give = expert(batch)
        sums.append((keep, move(give, swap)))

    def chip_sum(index, start, stop):
        keep, got = sums[index]
        return keep[start:stop].astype(jnp.float32) + got[start:stop].astype(jnp.float32)

    back_left = back_right = None
    if opposite:
        index = full_steps + 1
        back_left = move(chip_sum(index, 0, half).astype(jnp.bfloat16), left)
        back_right = move(chip_sum(index, half, rows).astype(jnp.bfloat16), right)
    for k in range(full_steps, 0, -1):
        to_left, to_right = chip_sum(k, 0, rows), chip_sum(k, rows, 2 * rows)
        if back_left is not None:
            if back_left.shape[0] == rows:
                to_left += back_left.astype(jnp.float32)
                to_right += back_right.astype(jnp.float32)
            else:
                to_left = jnp.concatenate([to_left[:half] + back_left.astype(jnp.float32), to_left[half:]])
                to_right = jnp.concatenate([to_right[:half], to_right[half:] + back_right.astype(jnp.float32)])
        back_left = move(to_left.astype(jnp.bfloat16), left)
        back_right = move(to_right.astype(jnp.bfloat16), right)
    total = resid.astype(jnp.float32) + chip_sum(0, 0, rows)
    if back_left is not None:
        if back_left.shape[0] == rows:
            total += back_left.astype(jnp.float32) + back_right.astype(jnp.float32)
        else:
            total += jnp.concatenate([back_left, back_right]).astype(jnp.float32)
    return total.astype(jnp.bfloat16)


def solution(mesh):
    in_specs = (
        P(("groups", "ep"), None),
        P(),
        P(("groups", "ep"), None),
        P(("groups", "ep"), None),
        P("ep", None, None),
        P("ep", None, None),
    )
    out_specs = P(("groups", "ep"), None)
    return jax.shard_map(local, mesh=mesh, in_specs=in_specs, out_specs=out_specs, check_vma=False)
```

```python
import functools

import jax
import jax.numpy as jnp
from jax import lax
from jax.experimental import pallas as pl
from jax.experimental.pallas import tpu as pltpu
from jax.sharding import PartitionSpec as P

LANES = 128
CORES = 2
CHUNKS = 2


def pack_kernel(experts, resid_ref, gain_ref, ids_ref, route_ref, out_ref):
    rows, width = resid_ref.shape
    lanes = out_ref.shape[1] - width
    wide = resid_ref[...].astype(jnp.float32)
    scale = lax.rsqrt(jnp.mean(wide * wide, axis=-1, keepdims=True) + 1e-06)
    out_ref[:, :width] = (wide * scale * gain_ref[...]).astype(jnp.bfloat16)
    route = route_ref[...]
    mix = route / jnp.sum(route, axis=-1, keepdims=True)
    ids = ids_ref[...]
    lane = lax.broadcasted_iota(jnp.int32, (rows, lanes), 1)
    expert = jnp.where(lane < experts, lane, lane - experts)
    table = jnp.zeros((rows, lanes), jnp.float32)
    for k in range(ids.shape[1]):
        table += jnp.where(ids[:, k : k + 1] == expert, mix[:, k : k + 1], 0.0)
    high = table.astype(jnp.bfloat16)
    low = (table - high.astype(jnp.float32)).astype(jnp.bfloat16)
    out_ref[:, width:] = jnp.where(lane < experts, high.astype(jnp.float32), low.astype(jnp.float32)).astype(
        jnp.bfloat16
    )


def pack(resid, norm_gain, expert_ids, route_weights, experts):
    rows, width = resid.shape
    lanes = -(-2 * experts // LANES) * LANES
    return pl.pallas_call(
        functools.partial(pack_kernel, experts),
        out_shape=jax.ShapeDtypeStruct((rows, width + lanes), jnp.bfloat16),
        compiler_params=pltpu.CompilerParams(vmem_limit_bytes=32 * 2**20),
        name="pack_rows",
    )(resid, norm_gain.reshape(1, width), expert_ids, route_weights)


def expert_kernel(experts, hidden_steps, own_ref, block_ref, gate_ref, up_ref, down_ref, out_ref, rows_ref, active_ref, weight_ref):
    step = pl.program_id(0)
    total, width = rows_ref.shape
    tile = gate_ref.shape[1]

    @pl.when(step == 0)
    def _():
        rows_ref[...] = block_ref[:, :width]
        table = block_ref[:, width:].astype(jnp.float32)
        lane = lax.broadcasted_iota(jnp.int32, table.shape, 1)
        mine = (lane == own_ref[0]) | (lane == own_ref[0] + experts)
        weight = jnp.sum(jnp.where(mine, table, 0.0), axis=1, keepdims=True)
        weight_ref[...] = jnp.broadcast_to(weight, (total, LANES))

    @pl.when(step < hidden_steps)
    def _():
        rows = rows_ref[...]
        gate = jnp.dot(rows, gate_ref[...], preferred_element_type=jnp.float32)
        up = jnp.dot(rows, up_ref[...], preferred_element_type=jnp.float32)
        value = (gate / (1.0 + jnp.exp(-gate)) * up).astype(jnp.bfloat16)
        for j in range(hidden_steps):

            @pl.when(step == j)
            def _():
                active_ref[:, j * tile : (j + 1) * tile] = value

    @pl.when(step >= hidden_steps)
    def _():
        produced = jnp.dot(active_ref[...], down_ref[...], preferred_element_type=jnp.float32)
        produced = produced.astype(jnp.bfloat16).astype(jnp.float32)
        weight = weight_ref[:, :1]
        out_ref[...] = jnp.where(weight == 0.0, 0.0, produced * weight).astype(jnp.bfloat16)


def apply_expert(own, block, w_in, w_out, experts):
    hidden, width = w_out.shape[1:]
    total, packed = block.shape
    tile = 256 if hidden % 256 == 0 else LANES
    hidden_steps = hidden // tile
    out_tile = 512 if width % 512 == 0 else LANES
    out_steps = width // out_tile
    late = lambda j: jnp.maximum(j - hidden_steps, 0)
    early = lambda j: jnp.minimum(j, hidden_steps - 1)
    return pl.pallas_call(
        functools.partial(expert_kernel, experts, hidden_steps),
        grid=(hidden_steps + out_steps,),
        in_specs=[
            pl.BlockSpec(memory_space=pltpu.SMEM),
            pl.BlockSpec(block.shape, lambda j: (0, 0)),
            pl.BlockSpec((None, width, tile), lambda j: (0, 0, early(j))),
            pl.BlockSpec((None, width, tile), lambda j: (0, 0, early(j) + hidden_steps)),
            pl.BlockSpec((None, hidden, out_tile), lambda j: (0, 0, late(j))),
        ],
        out_specs=pl.BlockSpec((total, out_tile), lambda j: (0, late(j))),
        out_shape=jax.ShapeDtypeStruct((total, width), jnp.bfloat16),
        scratch_shapes=[
            pltpu.VMEM((total, width), jnp.bfloat16),
            pltpu.VMEM((total, hidden), jnp.bfloat16),
            pltpu.VMEM((total, LANES), jnp.float32),
        ],
        compiler_params=pltpu.CompilerParams(
            dimension_semantics=("arbitrary",), vmem_limit_bytes=40 * 2**20
        ),
        cost_estimate=pl.CostEstimate(
            flops=6 * total * width * hidden,
            bytes_accessed=6 * width * hidden + 2 * total * (packed + width),
            transcendentals=total * hidden,
        ),
        name="expert_rows",
    )(own, block, w_in, w_in, w_out)


def local(resid, norm_gain, expert_ids, route_weights, w_in, w_out):
    rows, width = resid.shape
    devices = lax.axis_size("ep")
    chips = devices // CORES
    swap = [(i, i + 1 - 2 * (i % CORES)) for i in range(devices)]
    same_core = [[chip * CORES + core for chip in range(chips)] for core in range(CORES)]
    own = lax.axis_index("ep").reshape(1).astype(jnp.int32)
    part = rows // CHUNKS

    block = pack(resid, norm_gain, expert_ids, route_weights, devices)
    gathered = [
        lax.all_gather(block[c * part : (c + 1) * part], "ep", axis_index_groups=same_core, axis=0, tiled=True)
        for c in range(CHUNKS)
    ]
    back = []
    for mine in gathered:
        other = lax.ppermute(mine, "ep", swap)
        keep = apply_expert(own, mine, w_in, w_out, devices)
        give = apply_expert(own, other, w_in, w_out, devices)
        got = lax.ppermute(give, "ep", swap)
        both = (keep.astype(jnp.float32) + got.astype(jnp.float32)).astype(jnp.bfloat16)
        back.append(
            lax.psum_scatter(both, "ep", axis_index_groups=same_core, scatter_dimension=0, tiled=True)
        )
    mixed = jnp.concatenate(back).astype(jnp.float32)
    return (resid.astype(jnp.float32) + mixed).astype(jnp.bfloat16)


def solution(mesh):
    in_specs = (
        P(("groups", "ep"), None),
        P(),
        P(("groups", "ep"), None),
        P(("groups", "ep"), None),
        P("ep", None, None),
        P("ep", None, None),
    )
    out_specs = P(("groups", "ep"), None)
    return jax.shard_map(local, mesh=mesh, in_specs=in_specs, out_specs=out_specs, check_vma=False)
```

```python
import functools

import jax
import jax.numpy as jnp
from jax import lax
from jax.experimental import pallas as pl
from jax.experimental.pallas import tpu as pltpu
from jax.sharding import PartitionSpec as P

LANES = 128
CORES = 2


def ring_of(chips):
    return list(range(0, chips, 2)) + list(range(1, chips, 2))[::-1]


def permutations_of(chips):
    order = ring_of(chips)
    first, second, swap = [], [], []
    for place, chip in enumerate(order):
        after, before = order[(place + 1) % chips], order[(place - 1) % chips]
        first += [(chip * CORES, after * CORES), (chip * CORES + 1, before * CORES + 1)]
        second += [(chip * CORES, before * CORES), (chip * CORES + 1, after * CORES + 1)]
        swap += [(chip * CORES, chip * CORES + 1), (chip * CORES + 1, chip * CORES)]
    return first, second, swap


def expert_kernel(starts, tile, out_tile, column_ref, *refs):
    count = len(starts)
    blocks = refs[:count]
    gain_ref, mix_ref, in_ref, down_ref, keep_ref, give_ref, rows_ref, active_ref, weight_ref = refs[count:]
    total, width = rows_ref.shape
    hidden = active_ref.shape[1]
    half = total // 2
    chunk = 32
    start = 0
    for n, block in enumerate(blocks):
        size = block.shape[0]
        table = mix_ref[starts[n] : starts[n] + size, :]
        lane = lax.broadcasted_iota(jnp.int32, table.shape, 1)
        weight = jnp.sum(jnp.where(lane == column_ref[n], table, 0.0), axis=1, keepdims=True)
        weight_ref[start : start + size, :] = jnp.broadcast_to(weight, (size, LANES))

        def normalise(i, carry, block=block, start=start):
            here = pl.multiple_of(i * chunk, chunk)
            wide = block[pl.ds(here, chunk), :].astype(jnp.float32)
            scale = lax.rsqrt(jnp.mean(wide * wide, axis=-1, keepdims=True) + 1e-06)
            rows_ref[pl.ds(pl.multiple_of(start + here, chunk), chunk), :] = (wide * scale * gain_ref[...]).astype(
                jnp.bfloat16
            )
            return carry

        lax.fori_loop(0, size // chunk, normalise, 0)
        start += size

    def activate(j, carry):
        gate_at = pl.multiple_of(j * tile, tile)
        up_at = pl.multiple_of(hidden + j * tile, tile)
        rows = rows_ref[...]
        gate = jnp.dot(rows, in_ref[0, :, pl.ds(gate_at, tile)], preferred_element_type=jnp.float32)
        up = jnp.dot(rows, in_ref[0, :, pl.ds(up_at, tile)], preferred_element_type=jnp.float32)
        active_ref[:, pl.ds(gate_at, tile)] = (gate / (1.0 + jnp.exp(-gate)) * up).astype(jnp.bfloat16)
        return carry

    lax.fori_loop(0, hidden // tile, activate, 0)

    def produce(j, carry):
        at = pl.multiple_of(j * out_tile, out_tile)
        produced = jnp.dot(active_ref[...], down_ref[0, :, pl.ds(at, out_tile)], preferred_element_type=jnp.float32)
        produced = produced.astype(jnp.bfloat16).astype(jnp.float32)
        weight = weight_ref[:, :1]
        mixed = jnp.where(weight == 0.0, 0.0, produced * weight).astype(jnp.bfloat16)
        keep_ref[:, pl.ds(at, out_tile)] = mixed[:half]
        give_ref[:, pl.ds(at, out_tile)] = mixed[half:]
        return carry

    lax.fori_loop(0, width // out_tile, produce, 0)


def apply_expert(columns, blocks, starts, gain, mix, w_in, w_out):
    hidden, width = w_out.shape[1:]
    total = sum(block.shape[0] for block in blocks)
    tile = 256 if hidden % 256 == 0 else LANES
    out_tile = 512 if width % 512 == 0 else LANES
    whole = pl.BlockSpec(memory_space=pltpu.VMEM)
    return pl.pallas_call(
        functools.partial(expert_kernel, starts, tile, out_tile),
        in_specs=[pl.BlockSpec(memory_space=pltpu.SMEM)] + [whole] * (len(blocks) + 4),
        out_specs=[whole] * 2,
        out_shape=[jax.ShapeDtypeStruct((total // 2, width), jnp.bfloat16)] * 2,
        scratch_shapes=[
            pltpu.VMEM((total, width), jnp.bfloat16),
            pltpu.VMEM((total, hidden), jnp.bfloat16),
            pltpu.VMEM((total, LANES), jnp.float32),
        ],
        compiler_params=pltpu.CompilerParams(vmem_limit_bytes=VMEM_BYTES),
        cost_estimate=pl.CostEstimate(
            flops=6 * total * width * hidden,
            bytes_accessed=6 * width * hidden + 4 * total * width,
            transcendentals=total * hidden,
        ),
        name="expert_rows",
    )(columns, *blocks, gain, mix, w_in, w_out)


VMEM_BYTES = 40 * 2**20


def mix_tables(expert_ids, route_weights, swap, devices, own):
    mix = route_weights / jnp.sum(route_weights, axis=-1, keepdims=True)
    experts = jnp.arange(devices, dtype=jnp.int32)
    hits = expert_ids.T[None, :, :] == experts[:, None, None]
    table = jnp.sum(jnp.where(hits, mix.T[None, :, :], 0.0), axis=1)[None]
    if devices & (devices - 1):
        everything = lax.all_gather(table[0], "ep", axis=0)
        return lax.dynamic_index_in_dim(everything, own, axis=1, keepdims=False).T
    reach = 1
    while reach < devices:
        partner = [(i, i ^ reach) for i in range(devices)]
        table = jnp.concatenate([table, lax.ppermute(table, "ep", partner)])
        reach *= 2
    return lax.dynamic_index_in_dim(table, own, axis=1, keepdims=False).T


def local(resid, norm_gain, expert_ids, route_weights, w_in, w_out):
    rows, width = resid.shape
    devices = lax.axis_size("ep")
    chips = devices // CORES
    first, second, swap = permutations_of(chips)
    own = lax.axis_index("ep").astype(jnp.int32)
    half = rows // 2
    full_steps = (chips - 1) // 2
    opposite = chips % 2 == 0
    gain = norm_gain.reshape(1, width)

    def move(array, perm):
        return lax.ppermute(array, "ep", perm)

    order = ring_of(chips)
    place_of = {chip: place for place, chip in enumerate(order)}

    def sources(k):
        table = []
        for device in range(devices):
            chip, core = divmod(device, CORES)
            way = 1 if core == 0 else -1
            table.append(order[(place_of[chip] - way * k) % chips] * CORES + core)
        return table

    def columns_of(steps):
        table = []
        for device in range(devices):
            other = device + 1 - 2 * (device % CORES)
            mine = [sources(k)[device] for k in steps]
            shift = 0 if devices & (devices - 1) else device
            table.append([source ^ shift for source in mine + [sources(k)[other] for k in steps]])
        return lax.dynamic_index_in_dim(jnp.asarray(table, jnp.int32), own, axis=0, keepdims=False)

    mix = None

    def expert(steps, blocks, starts):
        return apply_expert(columns_of(steps), blocks, starts, gain, mix, w_in, w_out)

    def tie(*arrays):
        return lax.optimization_barrier(arrays)

    held = [(resid, resid)]
    swapped = {}
    results = {}

    def batch(k):
        if k == 0:
            return expert([0], [resid, swapped[0]], [0, 0])
        return expert([k, -k], [*held[k], *swapped[k]], [0, 0, 0, 0])

    for k in range(1, full_steps + 1):
        a, b = held[-1]
        went = move(a, first), move(b, second)
        if k == 1:
            swapped[0] = move(resid, swap)
            mix = mix_tables(expert_ids, route_weights, swap, devices, own)
        else:
            swapped[k - 1] = move(a, swap), move(b, swap)
            results[k - 2] = batch(k - 2)
            *went, keep, give = tie(*went, *results[k - 2])
            results[k - 2] = keep, give
        held.append(tuple(went))
    a, b = held[-1]
    if full_steps == 0:
        swapped[0] = move(resid, swap)
        mix = mix_tables(expert_ids, route_weights, swap, devices, own)
    else:
        swapped[full_steps] = move(a, swap), move(b, swap)
    far = None
    if opposite:
        far = move(a[:half], first), move(b[half:], second)
        if full_steps >= 1:
            results[full_steps - 1] = batch(full_steps - 1)
            *far, keep, give = tie(*far, *results[full_steps - 1])
            results[full_steps - 1] = keep, give
        far_swapped = move(far[0], swap), move(far[1], swap)
        steps = [full_steps + 1, -(full_steps + 1)]
        results[full_steps + 1] = expert(steps, [*far, *far_swapped], [0, half, 0, half])
    for k in range(full_steps + 1):
        if k not in results:
            results[k] = batch(k)

    got = {k: move(give, swap) for k, (_, give) in results.items()}

    def chip_sum(k, start, stop):
        return results[k][0][start:stop].astype(jnp.float32) + got[k][start:stop].astype(jnp.float32)

    back = None
    if opposite:
        k = full_steps + 1
        back = (
            move(chip_sum(k, 0, half).astype(jnp.bfloat16), second),
            move(chip_sum(k, half, rows).astype(jnp.bfloat16), first),
        )
    for k in range(full_steps, 0, -1):
        one, two = chip_sum(k, 0, rows), chip_sum(k, rows, 2 * rows)
        if back is not None:
            came = back[0].astype(jnp.float32), back[1].astype(jnp.float32)
            if k == full_steps:
                one = jnp.concatenate([one[:half] + came[0], one[half:]])
                two = jnp.concatenate([two[:half], two[half:] + came[1]])
            else:
                one, two = one + came[0], two + came[1]
        back = move(one.astype(jnp.bfloat16), second), move(two.astype(jnp.bfloat16), first)
    total = resid.astype(jnp.float32) + chip_sum(0, 0, rows)
    if back is not None:
        if full_steps == 0:
            total += jnp.concatenate(back).astype(jnp.float32)
        else:
            total += back[0].astype(jnp.float32) + back[1].astype(jnp.float32)
    return total.astype(jnp.bfloat16)


def solution(mesh):
    in_specs = (
        P(("groups", "ep"), None),
        P(),
        P(("groups", "ep"), None),
        P(("groups", "ep"), None),
        P("ep", None, None),
        P("ep", None, None),
    )
    out_specs = P(("groups", "ep"), None)
    return jax.shard_map(local, mesh=mesh, in_specs=in_specs, out_specs=out_specs, check_vma=False)
```

```python
import functools

import jax
import jax.numpy as jnp
from jax import lax
from jax.experimental import pallas as pl
from jax.experimental.pallas import tpu as pltpu
from jax.sharding import PartitionSpec as P

LANES = 128
CORES = 2


def ring_of(chips):
    return list(range(0, chips, 2)) + list(range(1, chips, 2))[::-1]


def permutations_of(chips):
    order = ring_of(chips)
    first, second, swap = [], [], []
    for place, chip in enumerate(order):
        after, before = order[(place + 1) % chips], order[(place - 1) % chips]
        first += [(chip * CORES, after * CORES), (chip * CORES + 1, before * CORES + 1)]
        second += [(chip * CORES, before * CORES), (chip * CORES + 1, after * CORES + 1)]
        swap += [(chip * CORES, chip * CORES + 1), (chip * CORES + 1, chip * CORES)]
    return first, second, swap


def pack_kernel(experts, resid_ref, gain_ref, ids_ref, route_ref, out_ref, *scratch):
    wide_ref, held_gain_ref, held_ids_ref, held_route_ref, sems = scratch
    pairs = zip((resid_ref, gain_ref, ids_ref, route_ref), scratch[:4])
    copies = [pltpu.make_async_copy(*pair, sems.at[n]) for n, pair in enumerate(pairs)]
    for copy in copies:
        copy.start()
    for copy in copies:
        copy.wait()
    rows, width = wide_ref.shape
    lanes = out_ref.shape[1] - width
    wide = wide_ref[...].astype(jnp.float32)
    scale = lax.rsqrt(jnp.mean(wide * wide, axis=-1, keepdims=True) + 1e-06)
    out_ref[:, :width] = (wide * scale * held_gain_ref[...]).astype(jnp.bfloat16)
    route = held_route_ref[...]
    mix = route / jnp.sum(route, axis=0, keepdims=True)
    ids = held_ids_ref[...]
    lane = lax.broadcasted_iota(jnp.int32, (lanes, rows), 0)
    expert = jnp.where(lane < experts, lane, lane - experts)
    table = jnp.zeros((lanes, rows), jnp.float32)
    for k in range(ids.shape[0]):
        table += jnp.where(ids[k : k + 1, :] == expert, mix[k : k + 1, :], 0.0)
    high = table.astype(jnp.bfloat16).astype(jnp.float32)
    out_ref[:, width:] = jnp.where(lane < experts, high, table - high).T.astype(jnp.bfloat16)


def pack(resid, norm_gain, expert_ids, route_weights, experts):
    rows, width = resid.shape
    top = expert_ids.shape[1]
    lanes = -(-2 * experts // LANES) * LANES
    return pl.pallas_call(
        functools.partial(pack_kernel, experts),
        in_specs=[pl.BlockSpec(memory_space=pltpu.HBM)] * 4,
        out_specs=pl.BlockSpec(memory_space=pltpu.VMEM),
        out_shape=jax.ShapeDtypeStruct((rows, width + lanes), jnp.bfloat16),
        scratch_shapes=[
            pltpu.VMEM((rows, width), jnp.bfloat16),
            pltpu.VMEM((1, width), jnp.float32),
            pltpu.VMEM((top, rows), jnp.int32),
            pltpu.VMEM((top, rows), jnp.float32),
            pltpu.SemaphoreType.DMA((4,)),
        ],
        compiler_params=pltpu.CompilerParams(vmem_limit_bytes=60 * 2**20),
        name="pack_rows",
    )(resid, norm_gain.reshape(1, width), expert_ids.T, route_weights.T)


def expert_kernel(experts, tile, out_tile, own_ref, *refs):
    *blocks, in_ref, down_ref, keep_ref, give_ref, rows_ref, active_ref, weight_ref = refs
    total, width = rows_ref.shape
    hidden = active_ref.shape[1]
    half = total // 2
    start = 0
    for block in blocks:
        size = block.shape[0]
        rows_ref[start : start + size, :] = block[:, :width]
        table = block[:, width:].astype(jnp.float32)
        lane = lax.broadcasted_iota(jnp.int32, table.shape, 1)
        mine = (lane == own_ref[0]) | (lane == own_ref[0] + experts)
        weight = jnp.sum(jnp.where(mine, table, 0.0), axis=1, keepdims=True)
        weight_ref[start : start + size, :] = jnp.broadcast_to(weight, (size, LANES))
        start += size

    for j in range(0, hidden, tile):
        rows = rows_ref[...]
        gate = jnp.dot(rows, in_ref[0, :, j : j + tile], preferred_element_type=jnp.float32)
        up = jnp.dot(rows, in_ref[0, :, hidden + j : hidden + j + tile], preferred_element_type=jnp.float32)
        active_ref[:, j : j + tile] = (gate / (1.0 + jnp.exp(-gate)) * up).astype(jnp.bfloat16)

    for j in range(0, width, out_tile):
        produced = jnp.dot(active_ref[...], down_ref[0, :, j : j + out_tile], preferred_element_type=jnp.float32)
        produced = produced.astype(jnp.bfloat16).astype(jnp.float32)
        weight = weight_ref[:, :1]
        mixed = jnp.where(weight == 0.0, 0.0, produced * weight).astype(jnp.bfloat16)
        keep_ref[:, j : j + out_tile] = mixed[:half]
        give_ref[:, j : j + out_tile] = mixed[half:]


def apply_expert(own, blocks, w_in, w_out, experts):
    hidden, width = w_out.shape[1:]
    total = sum(block.shape[0] for block in blocks)
    tile = 256 if hidden % 256 == 0 else LANES
    out_tile = 512 if width % 512 == 0 else LANES
    whole = pl.BlockSpec(memory_space=pltpu.VMEM)
    return pl.pallas_call(
        functools.partial(expert_kernel, experts, tile, out_tile),
        in_specs=[pl.BlockSpec(memory_space=pltpu.SMEM)] + [whole] * (len(blocks) + 2),
        out_specs=[whole] * 2,
        out_shape=[jax.ShapeDtypeStruct((total // 2, width), jnp.bfloat16)] * 2,
        scratch_shapes=[
            pltpu.VMEM((total, width), jnp.bfloat16),
            pltpu.VMEM((total, hidden), jnp.bfloat16),
            pltpu.VMEM((total, LANES), jnp.float32),
        ],
        compiler_params=pltpu.CompilerParams(vmem_limit_bytes=VMEM_BYTES),
        cost_estimate=pl.CostEstimate(
            flops=6 * total * width * hidden,
            bytes_accessed=6 * width * hidden + 4 * total * width,
            transcendentals=total * hidden,
        ),
        name="expert_rows",
    )(own, *blocks, w_in, w_out)


VMEM_BYTES = 16 * 2**20


def local(resid, norm_gain, expert_ids, route_weights, w_in, w_out):
    rows, width = resid.shape
    devices = lax.axis_size("ep")
    chips = devices // CORES
    first, second, swap = permutations_of(chips)
    own = lax.axis_index("ep").reshape(1).astype(jnp.int32)
    full_steps = (chips - 1) // 2
    opposite = chips % 2 == 0

    def move(array, perm):
        return lax.ppermute(array, "ep", perm)

    def expert(blocks):
        return apply_expert(own, blocks, w_in, w_out, devices)

    block = pack(resid, norm_gain, expert_ids, route_weights, devices)
    held = [[block]]
    blocks_of = []
    results = []
    steps = full_steps + 1 if opposite else full_steps
    for k in range(1, steps + 1):
        went = [move(held[-1][0], first)]
        if k <= full_steps:
            went.append(move(held[-1][-1], second))
        blocks_of.append(held[-1] + [move(part, swap) for part in held[-1]])
        pair = expert(blocks_of[k - 1])
        *went, keep, give = lax.optimization_barrier((*went, *pair))
        results.append((keep, give))
        held.append(went)
    blocks_of.append(held[-1] + [move(part, swap) for part in held[-1]])
    while len(results) < len(blocks_of):
        blocks = blocks_of[len(results)]
        if results:
            *blocks, keep, give = lax.optimization_barrier((*blocks, *results[-1]))
            results[-1] = keep, give
        results.append(expert(blocks))

    got = [move(give, swap) for _, give in results]

    def chip_sum(k, start):
        part = slice(start, start + rows)
        return results[k][0][part].astype(jnp.float32) + got[k][part].astype(jnp.float32)

    one = two = None
    for k in range(steps, -1, -1):
        sums = [chip_sum(k, n * rows) for n in range(len(held[k]))]
        if one is not None:
            sums[0] += one.astype(jnp.float32)
        if two is not None:
            sums[-1] += two.astype(jnp.float32)
        if k == 0:
            return (resid.astype(jnp.float32) + sums[0]).astype(jnp.bfloat16)
        one = move(sums[0].astype(jnp.bfloat16), second)
        two = move(sums[1].astype(jnp.bfloat16), first) if len(sums) > 1 else None


def solution(mesh):
    in_specs = (
        P(("groups", "ep"), None),
        P(),
        P(("groups", "ep"), None),
        P(("groups", "ep"), None),
        P("ep", None, None),
        P("ep", None, None),
    )
    out_specs = P(("groups", "ep"), None)
    return jax.shard_map(local, mesh=mesh, in_specs=in_specs, out_specs=out_specs, check_vma=False)
```

```python
import functools

import jax
import jax.numpy as jnp
from jax import lax
from jax.experimental import pallas as pl
from jax.experimental.pallas import tpu as pltpu
from jax.sharding import PartitionSpec as P

LANES = 128
CORES = 2
CHUNKS = 2


def ring_of(chips):
    return list(range(0, chips, 2)) + list(range(1, chips, 2))[::-1]


def permutations_of(chips):
    order = ring_of(chips)
    right, left, swap = [], [], []
    for place, chip in enumerate(order):
        after = order[(place + 1) % chips]
        for core in range(CORES):
            right.append((chip * CORES + core, after * CORES + core))
            left.append((after * CORES + core, chip * CORES + core))
            swap.append((chip * CORES + core, chip * CORES + 1 - core))
    return right, left, swap


def pack_kernel(experts, resid_ref, gain_ref, ids_ref, route_ref, *refs):
    *outs, wide_ref, held_gain_ref, held_ids_ref, held_route_ref, sems = refs
    held = (wide_ref, held_gain_ref, held_ids_ref, held_route_ref)
    pairs = zip((resid_ref, gain_ref, ids_ref, route_ref), held)
    copies = [pltpu.make_async_copy(*pair, sems.at[n]) for n, pair in enumerate(pairs)]
    for copy in copies:
        copy.start()
    for copy in copies:
        copy.wait()
    rows, width = wide_ref.shape
    part, lanes = rows // len(outs), outs[0].shape[1] - width
    route = held_route_ref[...]
    mix = route / jnp.sum(route, axis=0, keepdims=True)
    ids = held_ids_ref[...]
    lane = lax.broadcasted_iota(jnp.int32, (lanes, rows), 0)
    expert = jnp.where(lane < experts, lane, lane - experts)
    table = jnp.zeros((lanes, rows), jnp.float32)
    for k in range(ids.shape[0]):
        table += jnp.where(ids[k : k + 1, :] == expert, mix[k : k + 1, :], 0.0)
    high = table.astype(jnp.bfloat16).astype(jnp.float32)
    table = jnp.where(lane < experts, high, table - high).T.astype(jnp.bfloat16)
    for n, out_ref in enumerate(outs):
        wide = wide_ref[n * part : (n + 1) * part, :].astype(jnp.float32)
        scale = lax.rsqrt(jnp.mean(wide * wide, axis=-1, keepdims=True) + 1e-06)
        out_ref[:, :width] = (wide * scale * held_gain_ref[...]).astype(jnp.bfloat16)
        out_ref[:, width:] = table[n * part : (n + 1) * part]


def pack(resid, norm_gain, expert_ids, route_weights, experts):
    rows, width = resid.shape
    top = expert_ids.shape[1]
    lanes = -(-2 * experts // LANES) * LANES
    return pl.pallas_call(
        functools.partial(pack_kernel, experts),
        in_specs=[pl.BlockSpec(memory_space=pltpu.HBM)] * 4,
        out_specs=[pl.BlockSpec(memory_space=pltpu.VMEM)] * CHUNKS,
        out_shape=[jax.ShapeDtypeStruct((rows // CHUNKS, width + lanes), jnp.bfloat16)] * CHUNKS,
        scratch_shapes=[
            pltpu.VMEM((rows, width), jnp.bfloat16),
            pltpu.VMEM((1, width), jnp.float32),
            pltpu.VMEM((top, rows), jnp.int32),
            pltpu.VMEM((top, rows), jnp.float32),
            pltpu.SemaphoreType.DMA((4,)),
        ],
        compiler_params=pltpu.CompilerParams(vmem_limit_bytes=60 * 2**20),
        name="pack_rows",
    )(resid, norm_gain.reshape(1, width), expert_ids.T, route_weights.T)


def expert_kernel(experts, tile, out_tile, own_ref, *refs):
    *blocks, in_ref, down_ref, keep_ref, give_ref, rows_ref, active_ref, weight_ref = refs
    total, width = rows_ref.shape
    hidden = active_ref.shape[1]
    half = total // 2
    start = 0
    for block in blocks:
        size = block.shape[0]
        rows_ref[start : start + size, :] = block[:, :width]
        table = block[:, width:].astype(jnp.float32)
        lane = lax.broadcasted_iota(jnp.int32, table.shape, 1)
        mine = (lane == own_ref[0]) | (lane == own_ref[0] + experts)
        weight = jnp.sum(jnp.where(mine, table, 0.0), axis=1, keepdims=True)
        weight_ref[start : start + size, :] = jnp.broadcast_to(weight, (size, LANES))
        start += size

    for j in range(0, hidden, tile):
        rows = rows_ref[...]
        gate = jnp.dot(rows, in_ref[0, :, j : j + tile], preferred_element_type=jnp.float32)
        up = jnp.dot(rows, in_ref[0, :, hidden + j : hidden + j + tile], preferred_element_type=jnp.float32)
        active_ref[:, j : j + tile] = (gate / (1.0 + jnp.exp(-gate)) * up).astype(jnp.bfloat16)

    for j in range(0, width, out_tile):
        produced = jnp.dot(active_ref[...], down_ref[0, :, j : j + out_tile], preferred_element_type=jnp.float32)
        produced = produced.astype(jnp.bfloat16).astype(jnp.float32)
        weight = weight_ref[:, :1]
        mixed = jnp.where(weight == 0.0, 0.0, produced * weight).astype(jnp.bfloat16)
        keep_ref[:, j : j + out_tile] = mixed[:half]
        give_ref[:, j : j + out_tile] = mixed[half:]


def apply_expert(own, blocks, w_in, w_out, experts):
    hidden, width = w_out.shape[1:]
    total = sum(block.shape[0] for block in blocks)
    tile = 256 if hidden % 256 == 0 else LANES
    out_tile = 512 if width % 512 == 0 else LANES
    whole = pl.BlockSpec(memory_space=pltpu.VMEM)
    return pl.pallas_call(
        functools.partial(expert_kernel, experts, tile, out_tile),
        in_specs=[pl.BlockSpec(memory_space=pltpu.SMEM)] + [whole] * (len(blocks) + 2),
        out_specs=[whole] * 2,
        out_shape=[jax.ShapeDtypeStruct((total // 2, width), jnp.bfloat16)] * 2,
        scratch_shapes=[
            pltpu.VMEM((total, width), jnp.bfloat16),
            pltpu.VMEM((total, hidden), jnp.bfloat16),
            pltpu.VMEM((total, LANES), jnp.float32),
        ],
        compiler_params=pltpu.CompilerParams(vmem_limit_bytes=VMEM_BYTES),
        cost_estimate=pl.CostEstimate(
            flops=6 * total * width * hidden,
            bytes_accessed=6 * width * hidden + 4 * total * width,
            transcendentals=total * hidden,
        ),
        name="expert_rows",
    )(own, *blocks, w_in, w_out)


VMEM_BYTES = 16 * 2**20


def local(resid, norm_gain, expert_ids, route_weights, w_in, w_out):
    rows = resid.shape[0] // CHUNKS
    devices = lax.axis_size("ep")
    chips = devices // CORES
    right, left, swap = permutations_of(chips)
    own = lax.axis_index("ep").reshape(1).astype(jnp.int32)
    full_steps = (chips - 1) // 2
    steps = chips // 2

    def move(array, perm):
        return lax.ppermute(array, "ep", perm)

    last = []

    def expert(blocks):
        blocks = lax.optimization_barrier((*blocks, *last))[: len(blocks)]
        last[:] = apply_expert(own, blocks, w_in, w_out, devices)
        return tuple(last)

    ways = [(right, left), (left, right)] * CHUNKS
    held = [[[block]] for block in pack(resid, norm_gain, expert_ids, route_weights, devices)]
    blocks_of = [[] for _ in held]
    results = [[] for _ in held]
    for k in range(1, steps + 2):
        for c, (first, second) in zip(range(CHUNKS), ways):
            here = held[c][-1]
            went = []
            if k <= steps:
                went.append(move(here[0], first))
            if k <= full_steps:
                went.append(move(here[-1], second))
            pair = expert(here + [move(part, swap) for part in here])
            if went:
                *went, keep, give = lax.optimization_barrier((*went, *pair))
                pair = keep, give
            results[c].append(pair)
            held[c].append(went)

    outs = []
    for c, (first, second) in zip(range(CHUNKS), ways):
        got = [move(give, swap) for _, give in results[c]]

        def chip_sum(k, start):
            part = slice(start, start + rows)
            return results[c][k][0][part].astype(jnp.float32) + got[k][part].astype(jnp.float32)

        one = two = None
        for k in range(steps, 0, -1):
            sums = [chip_sum(k, n * rows) for n in range(len(held[c][k]))]
            if one is not None:
                sums[0] += one.astype(jnp.float32)
            if two is not None:
                sums[-1] += two.astype(jnp.float32)
            one = move(sums[0].astype(jnp.bfloat16), second)
            two = move(sums[1].astype(jnp.bfloat16), first) if len(sums) > 1 else None
        total = resid[c * rows : (c + 1) * rows].astype(jnp.float32) + chip_sum(0, 0)
        for came in (one, two):
            if came is not None:
                total += came.astype(jnp.float32)
        outs.append(total.astype(jnp.bfloat16))
    return jnp.concatenate(outs)


def solution(mesh):
    in_specs = (
        P(("groups", "ep"), None),
        P(),
        P(("groups", "ep"), None),
        P(("groups", "ep"), None),
        P("ep", None, None),
        P("ep", None, None),
    )
    out_specs = P(("groups", "ep"), None)
    return jax.shard_map(local, mesh=mesh, in_specs=in_specs, out_specs=out_specs, check_vma=False)
```

```python
import functools

import jax
import jax.numpy as jnp
from jax import lax
from jax.experimental import pallas as pl
from jax.experimental.pallas import tpu as pltpu
from jax.sharding import PartitionSpec as P

LANES = 128
CORES = 2


def ring_of(chips):
    return list(range(0, chips, 2)) + list(range(1, chips, 2))[::-1]


def permutations_of(chips):
    order = ring_of(chips)

    def forward(hops):
        return [
            (chip * CORES + core, order[(place + hops) % chips] * CORES + core)
            for place, chip in enumerate(order)
            for core in range(CORES)
        ]

    swap = [(device, device + 1 - 2 * (device % CORES)) for device in range(chips * CORES)]
    return forward, swap


def pack_kernel(experts, resid_ref, gain_ref, ids_ref, route_ref, out_ref, *scratch):
    wide_ref, held_gain_ref, held_ids_ref, held_route_ref, sems = scratch
    pairs = zip((resid_ref, gain_ref, ids_ref, route_ref), scratch[:4])
    copies = [pltpu.make_async_copy(*pair, sems.at[n]) for n, pair in enumerate(pairs)]
    for copy in copies:
        copy.start()
    for copy in copies:
        copy.wait()
    rows, width = wide_ref.shape
    lanes = out_ref.shape[1] - width
    wide = wide_ref[...].astype(jnp.float32)
    scale = lax.rsqrt(jnp.mean(wide * wide, axis=-1, keepdims=True) + 1e-06)
    out_ref[:, :width] = (wide * scale * held_gain_ref[...]).astype(jnp.bfloat16)
    route = held_route_ref[...]
    mix = route / jnp.sum(route, axis=0, keepdims=True)
    ids = held_ids_ref[...]
    lane = lax.broadcasted_iota(jnp.int32, (lanes, rows), 0)
    expert = jnp.where(lane < experts, lane, lane - experts)
    table = jnp.zeros((lanes, rows), jnp.float32)
    for k in range(ids.shape[0]):
        table += jnp.where(ids[k : k + 1, :] == expert, mix[k : k + 1, :], 0.0)
    high = table.astype(jnp.bfloat16).astype(jnp.float32)
    out_ref[:, width:] = jnp.where(lane < experts, high, table - high).T.astype(jnp.bfloat16)


def pack(resid, norm_gain, expert_ids, route_weights, experts):
    rows, width = resid.shape
    top = expert_ids.shape[1]
    lanes = -(-2 * experts // LANES) * LANES
    return pl.pallas_call(
        functools.partial(pack_kernel, experts),
        in_specs=[pl.BlockSpec(memory_space=pltpu.HBM)] * 4,
        out_specs=pl.BlockSpec(memory_space=pltpu.VMEM),
        out_shape=jax.ShapeDtypeStruct((rows, width + lanes), jnp.bfloat16),
        scratch_shapes=[
            pltpu.VMEM((rows, width), jnp.bfloat16),
            pltpu.VMEM((1, width), jnp.float32),
            pltpu.VMEM((top, rows), jnp.int32),
            pltpu.VMEM((top, rows), jnp.float32),
            pltpu.SemaphoreType.DMA((4,)),
        ],
        compiler_params=pltpu.CompilerParams(vmem_limit_bytes=60 * 2**20),
        name="pack_rows",
    )(resid, norm_gain.reshape(1, width), expert_ids.T, route_weights.T)


def expert_kernel(experts, tile, out_tile, own_ref, *refs):
    *blocks, in_ref, down_ref, keep_ref, give_ref, rows_ref, active_ref, weight_ref = refs
    total, width = rows_ref.shape
    hidden = active_ref.shape[1]
    half = total // 2
    start = 0
    for block in blocks:
        size = block.shape[0]
        rows_ref[start : start + size, :] = block[:, :width]
        table = block[:, width:].astype(jnp.float32)
        lane = lax.broadcasted_iota(jnp.int32, table.shape, 1)
        mine = (lane == own_ref[0]) | (lane == own_ref[0] + experts)
        weight = jnp.sum(jnp.where(mine, table, 0.0), axis=1, keepdims=True)
        weight_ref[start : start + size, :] = jnp.broadcast_to(weight, (size, LANES))
        start += size

    for j in range(0, hidden, tile):
        rows = rows_ref[...]
        gate = jnp.dot(rows, in_ref[0, :, j : j + tile], preferred_element_type=jnp.float32)
        up = jnp.dot(rows, in_ref[0, :, hidden + j : hidden + j + tile], preferred_element_type=jnp.float32)
        active_ref[:, j : j + tile] = (gate / (1.0 + jnp.exp(-gate)) * up).astype(jnp.bfloat16)

    for j in range(0, width, out_tile):
        produced = jnp.dot(active_ref[...], down_ref[0, :, j : j + out_tile], preferred_element_type=jnp.float32)
        produced = produced.astype(jnp.bfloat16).astype(jnp.float32)
        weight = weight_ref[:, :1]
        mixed = jnp.where(weight == 0.0, 0.0, produced * weight).astype(jnp.bfloat16)
        keep_ref[:, j : j + out_tile] = mixed[:half]
        give_ref[:, j : j + out_tile] = mixed[half:]


def apply_expert(own, blocks, w_in, w_out, experts):
    hidden, width = w_out.shape[1:]
    total = sum(block.shape[0] for block in blocks)
    tile = 256 if hidden % 256 == 0 else LANES
    out_tile = 512 if width % 512 == 0 else LANES
    whole = pl.BlockSpec(memory_space=pltpu.VMEM)
    return pl.pallas_call(
        functools.partial(expert_kernel, experts, tile, out_tile),
        in_specs=[pl.BlockSpec(memory_space=pltpu.SMEM)] + [whole] * (len(blocks) + 2),
        out_specs=[whole] * 2,
        out_shape=[jax.ShapeDtypeStruct((total // 2, width), jnp.bfloat16)] * 2,
        scratch_shapes=[
            pltpu.VMEM((total, width), jnp.bfloat16),
            pltpu.VMEM((total, hidden), jnp.bfloat16),
            pltpu.VMEM((total, LANES), jnp.float32),
        ],
        compiler_params=pltpu.CompilerParams(vmem_limit_bytes=VMEM_BYTES),
        cost_estimate=pl.CostEstimate(
            flops=6 * total * width * hidden,
            bytes_accessed=6 * width * hidden + 4 * total * width,
            transcendentals=total * hidden,
        ),
        name="expert_rows",
    )(own, *blocks, w_in, w_out)


VMEM_BYTES = 16 * 2**20


def local(resid, norm_gain, expert_ids, route_weights, w_in, w_out):
    rows = resid.shape[0]
    devices = lax.axis_size("ep")
    chips = devices // CORES
    forward, swap = permutations_of(chips)
    own = lax.axis_index("ep").reshape(1).astype(jnp.int32)
    half = rows // 2
    full_steps = (chips - 1) // 2
    opposite = chips % 2 == 0

    def move(array, hops):
        return lax.ppermute(array, "ep", forward(hops))

    def trade(array):
        return lax.ppermute(array, "ep", swap)

    def tie(first, second):
        out = lax.optimization_barrier((*first, *second))
        return list(out[: len(first)]), list(out[len(first) :])

    def expert(blocks):
        return list(apply_expert(own, blocks, w_in, w_out, devices))

    block = pack(resid, norm_gain, expert_ids, route_weights, devices)
    held = [[block]]
    results = []
    for k in range(1, full_steps + 2):
        if k <= full_steps:
            went = [move(held[-1][0], 1), move(held[-1][-1], -1)]
        elif opposite:
            went = [move(held[-1][0][:half], 1), move(held[-1][-1][half:], -1)]
        else:
            went = []
        blocks = held[-1] + [trade(part) for part in held[-1]]
        if results:
            results[-1], blocks = tie(results[-1], blocks)
        pair, went = tie(expert(blocks), went)
        results.append(pair)
        held.append(went)

    def chip_sum(keep, got, start, stop):
        return keep[start:stop].astype(jnp.float32) + got[start:stop].astype(jnp.float32)

    back = far = None
    for k in range(full_steps, -1, -1):
        keep, give = results[k]
        got = trade(give)
        sums = [chip_sum(keep, got, n * rows, (n + 1) * rows) for n in range(2 if k else 1)]
        if back is not None:
            sums[0] += back[0].astype(jnp.float32)
            sums[-1] += back[1].astype(jnp.float32)
        if far is not None and k == max(full_steps - 1, 0):
            zeros = jnp.zeros((half, sums[0].shape[1]), jnp.float32)
            sums[0] += jnp.concatenate([far[0].astype(jnp.float32), zeros])
            sums[-1] += jnp.concatenate([zeros, far[1].astype(jnp.float32)])
        if k:
            back = [part.astype(jnp.bfloat16) for part in sums]
        if opposite and k == full_steps:
            blocks = held[-1] + [trade(part) for part in held[-1]]
            if k:
                back, blocks = tie(back, blocks)
            keep, give = expert(blocks)
            got = trade(give)
            skip = min(full_steps, 1) + 1
            far = (
                move(chip_sum(keep, got, 0, half).astype(jnp.bfloat16), -skip),
                move(chip_sum(keep, got, half, rows).astype(jnp.bfloat16), skip),
            )
        if k:
            back = move(back[0], -1), move(back[1], 1)
    if full_steps == 0 and opposite:
        sums[0] += jnp.concatenate(far).astype(jnp.float32)
    return (resid.astype(jnp.float32) + sums[0]).astype(jnp.bfloat16)


def solution(mesh):
    in_specs = (
        P(("groups", "ep"), None),
        P(),
        P(("groups", "ep"), None),
        P(("groups", "ep"), None),
        P("ep", None, None),
        P("ep", None, None),
    )
    out_specs = P(("groups", "ep"), None)
    return jax.shard_map(local, mesh=mesh, in_specs=in_specs, out_specs=out_specs, check_vma=False)
```

```python
import functools

import jax
import jax.numpy as jnp
from jax import lax
from jax.experimental import pallas as pl
from jax.experimental.pallas import tpu as pltpu
from jax.sharding import PartitionSpec as P

LANES = 128
CORES = 2


def ring_of(chips):
    return list(range(0, chips, 2)) + list(range(1, chips, 2))[::-1]


def permutations_of(chips):
    order = ring_of(chips)

    def forward(hops):
        return [
            (chip * CORES + core, order[(place + hops) % chips] * CORES + core)
            for place, chip in enumerate(order)
            for core in range(CORES)
        ]

    swap = [(device, device + 1 - 2 * (device % CORES)) for device in range(chips * CORES)]
    return forward, swap


def pack_kernel(experts, resid_ref, gain_ref, ids_ref, route_ref, out_ref, *scratch):
    wide_ref, held_gain_ref, held_ids_ref, held_route_ref, sems = scratch
    pairs = zip((resid_ref, gain_ref, ids_ref, route_ref), scratch[:4])
    copies = [pltpu.make_async_copy(*pair, sems.at[n]) for n, pair in enumerate(pairs)]
    for copy in copies:
        copy.start()
    for copy in copies:
        copy.wait()
    rows, width = wide_ref.shape
    lanes = out_ref.shape[1] - width
    wide = wide_ref[...].astype(jnp.float32)
    scale = lax.rsqrt(jnp.mean(wide * wide, axis=-1, keepdims=True) + 1e-06)
    out_ref[:, :width] = (wide * scale * held_gain_ref[...]).astype(jnp.bfloat16)
    route = held_route_ref[...]
    mix = route / jnp.sum(route, axis=0, keepdims=True)
    ids = held_ids_ref[...]
    lane = lax.broadcasted_iota(jnp.int32, (lanes, rows), 0)
    expert = jnp.where(lane < experts, lane, lane - experts)
    table = jnp.zeros((lanes, rows), jnp.float32)
    for k in range(ids.shape[0]):
        table += jnp.where(ids[k : k + 1, :] == expert, mix[k : k + 1, :], 0.0)
    high = table.astype(jnp.bfloat16).astype(jnp.float32)
    out_ref[:, width:] = jnp.where(lane < experts, high, table - high).T.astype(jnp.bfloat16)


def pack(resid, norm_gain, expert_ids, route_weights, experts):
    rows, width = resid.shape
    top = expert_ids.shape[1]
    lanes = -(-2 * experts // LANES) * LANES
    return pl.pallas_call(
        functools.partial(pack_kernel, experts),
        in_specs=[pl.BlockSpec(memory_space=pltpu.HBM)] * 4,
        out_specs=pl.BlockSpec(memory_space=pltpu.VMEM),
        out_shape=jax.ShapeDtypeStruct((rows, width + lanes), jnp.bfloat16),
        scratch_shapes=[
            pltpu.VMEM((rows, width), jnp.bfloat16),
            pltpu.VMEM((1, width), jnp.float32),
            pltpu.VMEM((top, rows), jnp.int32),
            pltpu.VMEM((top, rows), jnp.float32),
            pltpu.SemaphoreType.DMA((4,)),
        ],
        compiler_params=pltpu.CompilerParams(vmem_limit_bytes=60 * 2**20),
        name="pack_rows",
    )(resid, norm_gain.reshape(1, width), expert_ids.T, route_weights.T)


def expert_kernel(experts, tile, out_tile, count, own_ref, *refs):
    blocks, refs = refs[:count], refs[count:]
    in_refs, down_refs, outs = refs[:CORES], refs[CORES : 2 * CORES], refs[2 * CORES : 2 * CORES + count]
    rows_ref, active_ref, weight_ref = refs[2 * CORES + count :]
    total, width = rows_ref.shape
    hidden = down_refs[0].shape[1]
    start = 0
    for block in blocks:
        size = block.shape[0]
        rows_ref[start : start + size, :] = block[:, :width]
        table = block[:, width:].astype(jnp.float32)
        lane = lax.broadcasted_iota(jnp.int32, table.shape, 1)
        for n in range(CORES):
            mine = (lane == own_ref[n]) | (lane == own_ref[n] + experts)
            weight = jnp.sum(jnp.where(mine, table, 0.0), axis=1, keepdims=True)
            weight_ref[n, start : start + size, :] = jnp.broadcast_to(weight, (size, LANES))
        start += size

    for n, in_ref in enumerate(in_refs):
        for j in range(0, hidden, tile):
            rows = rows_ref[...]
            gate = jnp.dot(rows, in_ref[0, :, j : j + tile], preferred_element_type=jnp.float32)
            up = jnp.dot(rows, in_ref[0, :, hidden + j : hidden + j + tile], preferred_element_type=jnp.float32)
            active_ref[n, :, j : j + tile] = (gate / (1.0 + jnp.exp(-gate)) * up).astype(jnp.bfloat16)

    for j in range(0, width, out_tile):
        mixed = jnp.zeros((total, out_tile), jnp.float32)
        for n, down_ref in enumerate(down_refs):
            produced = jnp.dot(active_ref[n], down_ref[0, :, j : j + out_tile], preferred_element_type=jnp.float32)
            produced = produced.astype(jnp.bfloat16).astype(jnp.float32)
            weight = weight_ref[n, :, :1]
            mixed += jnp.where(weight == 0.0, 0.0, produced * weight)
        start = 0
        for out in outs:
            size = out.shape[0]
            out[:, j : j + out_tile] = mixed[start : start + size].astype(jnp.bfloat16)
            start += size


def apply_experts(own, blocks, w_in, w_out, experts):
    hidden, width = w_out[0].shape[1:]
    total = sum(block.shape[0] for block in blocks)
    tile = 256 if hidden % 256 == 0 else LANES
    out_tile = 512 if width % 512 == 0 else LANES
    whole = pl.BlockSpec(memory_space=pltpu.VMEM)
    return pl.pallas_call(
        functools.partial(expert_kernel, experts, tile, out_tile, len(blocks)),
        in_specs=[pl.BlockSpec(memory_space=pltpu.SMEM)] + [whole] * (len(blocks) + 2 * CORES),
        out_specs=[whole] * len(blocks),
        out_shape=[jax.ShapeDtypeStruct((block.shape[0], width), jnp.bfloat16) for block in blocks],
        scratch_shapes=[
            pltpu.VMEM((total, width), jnp.bfloat16),
            pltpu.VMEM((CORES, total, hidden), jnp.bfloat16),
            pltpu.VMEM((CORES, total, LANES), jnp.float32),
        ],
        compiler_params=pltpu.CompilerParams(vmem_limit_bytes=VMEM_BYTES),
        cost_estimate=pl.CostEstimate(
            flops=CORES * 6 * total * width * hidden,
            bytes_accessed=CORES * 6 * width * hidden + 4 * total * width,
            transcendentals=CORES * total * hidden,
        ),
        name="expert_rows",
    )(own, *blocks, *w_in, *w_out)


VMEM_BYTES = 16 * 2**20


def local(resid, norm_gain, expert_ids, route_weights, w_in, w_out):
    rows = resid.shape[0]
    devices = lax.axis_size("ep")
    chips = devices // CORES
    forward, swap = permutations_of(chips)
    own = lax.axis_index("ep").astype(jnp.int32)
    own = jnp.stack([own, own + 1 - 2 * (own % CORES)])
    half = rows // 2
    full_steps = (chips - 1) // 2
    opposite = chips % 2 == 0

    def move(array, hops):
        return lax.ppermute(array, "ep", forward(hops))

    w_in = w_in, lax.ppermute(w_in, "ep", swap)
    w_out = w_out, lax.ppermute(w_out, "ep", swap)

    def tie(first, second):
        out = lax.optimization_barrier((*first, *second))
        return list(out[: len(first)]), list(out[len(first) :])

    def batch(blocks):
        return list(apply_experts(own, blocks, w_in, w_out, devices))

    block = pack(resid, norm_gain, expert_ids, route_weights, devices)
    held = [[block, block]]
    sums = [None]
    for k in range(1, full_steps + 2):
        if k <= full_steps:
            went = [move(held[-1][0], 1), move(held[-1][1], -1)]
        elif opposite:
            went = [move(held[-1][0][:half], 1), move(held[-1][1][half:], -1)]
        else:
            went = []
        if k > 1:
            done, went = tie(batch(held[-1]), went)
            sums.append(done)
        held.append(went)
    if opposite:
        sums.append(batch(held[-1]))

    back = [part for part in sums[-1]] if opposite else None
    if opposite:
        back = [move(back[0], -1), move(back[1], 1)]
    for k in range(full_steps, 0, -1):
        parts = [part.astype(jnp.float32) for part in sums[k]]
        if back is not None:
            came = [part.astype(jnp.float32) for part in back]
            if came[0].shape[0] < rows:
                parts[0] = jnp.concatenate([parts[0][:half] + came[0], parts[0][half:]])
                parts[1] = jnp.concatenate([parts[1][:half], parts[1][half:] + came[1]])
            else:
                parts = [part + other for part, other in zip(parts, came)]
        back = [move(parts[0].astype(jnp.bfloat16), -1), move(parts[1].astype(jnp.bfloat16), 1)]
        if k == full_steps:
            sums[0], back = tie(batch([block]), back)
    if sums[0] is None:
        sums[0] = batch([block])
    total = resid.astype(jnp.float32) + sums[0][0].astype(jnp.float32)
    if back is not None:
        came = [part.astype(jnp.float32) for part in back]
        total += jnp.concatenate(came) if came[0].shape[0] < rows else came[0] + came[1]
    return total.astype(jnp.bfloat16)


def solution(mesh):
    in_specs = (
        P(("groups", "ep"), None),
        P(),
        P(("groups", "ep"), None),
        P(("groups", "ep"), None),
        P("ep", None, None),
        P("ep", None, None),
    )
    out_specs = P(("groups", "ep"), None)
    return jax.shard_map(local, mesh=mesh, in_specs=in_specs, out_specs=out_specs, check_vma=False)
```
